512 devices in a mesh: bricks: 512 (over y, x, z, core).
Axes of the slice: x: 4, y: 4, z: 16, core: 2. Of those that a mesh axis runs over, the one named last changes fastest.
Arguments:
- density: bfloat16 [512, 4, 128, 256], P('bricks'), may hold values from -6 to 6
- material: int32 [512, 4, 128, 256], P('bricks'), may hold values from 0 to 7
- colour_table: float32 [8, 3], replicated, may hold values from 0.1 to 1
- opacity_table: float32 [8], replicated, may hold values from 0.002 to 0.04
- centre_table: float32 [8], replicated, may hold values from -1 to 1
- slice_weights: float32 [512, 4, 4], P('bricks'), may hold values from 0.1 to 1
- front_flags: int32 [512, 5], P('bricks'), may hold values from 0 to 1, as said below
Outputs:
- frame: float32 [4, 512, 2048], P(None, 'bricks')
The draws below stay inside these ranges and needn't reach their ends.
Inputs may be any that keep to these rules, and one draw needn't show every extreme that they name: `front_flags`: the last column is the same for every brick. Column k < 4 equals bit k of bx XOR that last column, with bx = brick index // 32.
All inputs are finite; a program needn't handle non-finite values.
Results may differ from the reference program's by a relative error of at most 0.0012.
Values may be sent and summed in bfloat16 or wider, within the bound.
A program may use at most 64 MiB of HBM per device.

```python
import math
import jax
import jax.numpy as jnp
from jax import lax

GX = 16
GZ = 2
ROUNDS = 4
MATS = 8
CX = 4
CY = 128
CZ = 256
BRICKS = 512
GY = 16


def draw_front_flags(key, part):
    key = jax.random.fold_in(key, 7)
    marching = jax.random.randint(key, (), 0, 2)
    indices = jnp.arange(BRICKS)
    position = indices // (BRICKS // GX)
    columns = []
    for which_bit in range(ROUNDS):
        bit_value = jnp.bitwise_and(jnp.right_shift(position, which_bit), 1)
        columns.append(jnp.bitwise_xor(bit_value, marching))
    columns.append(jnp.zeros_like(position) + marching)
    return jnp.stack(columns, axis=1).astype(jnp.int32)


def with_ends(values, stream_key, smallest, high):
    longest = values.shape.index(max(values.shape))
    spots = []
    for shift in (0, 1):
        where = [jax.random.randint(jax.random.fold_in(stream_key, axis), (), 0, length) for axis, length in enumerate(values.shape)]
        where[longest] = (where[longest] + shift) % values.shape[longest]
        spots.append(tuple(where))
    return values.at[spots[0]].set(smallest).at[spots[1]].set(high)


def block_scale(key, dims, split, low, top_value):
    factor_of = 1.0
    for axis_at, shards_of in split:
        heights = jax.random.uniform(jax.random.fold_in(jax.random.fold_in(key, 6), axis_at), (shards_of,), jnp.float32, low / len(split), top_value / len(split))
        factor_of = factor_of * jnp.repeat(jnp.exp(heights), dims[axis_at] // shards_of).reshape((-1,) + (1,) * (len(dims) - 1 - axis_at))
    return factor_of


def bell_draw(key, shape, deviation, most, cuts=(), dtype=jnp.bfloat16):
    drawn = jax.random.normal(key, shape, jnp.float32) * deviation
    if len(cuts) > 0:
        drawn = block_scale(key, shape, cuts, -0.22, 0.18) * drawn
    return jnp.clip(drawn, min=-most, max=most).astype(dtype)


def setup_inputs(seed: int = 0) -> dict:
    arg_keys = jax.random.split(jax.random.key(seed), 8)
    return {
        "density": bell_draw(arg_keys[0], (BRICKS, CX, CY, CZ), 1.0, 6.0, ((0, 512),)),
        "material": with_ends(jax.random.randint(arg_keys[1], (BRICKS, CX, CY, CZ), 0, MATS), jax.random.fold_in(arg_keys[1], 1), 0, MATS - 1).astype(jnp.int32),
        "colour_table": jnp.clip(jax.random.uniform(arg_keys[2], (MATS, 3), jnp.float32, 0.1, 1.0), 0.1, 1.0),
        "opacity_table": jnp.clip(jnp.exp(jax.random.uniform(arg_keys[3], (MATS,), jnp.float32, math.log(0.002), math.log(0.04))), 0.002, 0.04),
        "centre_table": jnp.clip(jax.random.uniform(arg_keys[4], (MATS,), jnp.float32, -1.0, 1.0), -1.0, 1.0),
        "slice_weights": jnp.clip(0.1 + 0.9 * jax.random.uniform(arg_keys[5], (BRICKS, CX, 4), jnp.float32) ** block_scale(arg_keys[5], (BRICKS, CX, 4), ((0, 512),), -0.2, 0.2), 0.1, 1.0),
        "front_flags": draw_front_flags(jax.random.fold_in(arg_keys[7], 71), 0),
    }


def classify(values, materials, grad_x, grad_y, grad_z, colour_table, opacity_table, centre_table):
    opacity = jnp.zeros_like(values)
    centre = jnp.zeros_like(values)
    tint_red = jnp.zeros_like(values)
    tint_green = jnp.zeros_like(values)
    tint_blue = jnp.zeros_like(values)
    for material_id in range(MATS):
        matched = materials == material_id
        opacity = jnp.where(matched, opacity_table[material_id], opacity)
        centre = jnp.where(matched, centre_table[material_id], centre)
        tint_red = jnp.where(matched, colour_table[material_id, 0], tint_red)
        tint_green = jnp.where(matched, colour_table[material_id, 1], tint_green)
        tint_blue = jnp.where(matched, colour_table[material_id, 2], tint_blue)
    absorb = opacity * jax.nn.sigmoid(2.0 * (values - centre))
    length = jnp.sqrt(grad_x * grad_x + grad_y * grad_y + grad_z * grad_z + 1.0)
    facing = jnp.abs(0.6 * grad_x + 0.48 * grad_y + 0.64 * grad_z) / length
    weight = (0.35 + 0.65 * facing) * absorb
    return jnp.stack([tint_red * weight, tint_green * weight, tint_blue * weight, absorb])

def resample(colours, weights):
    first = weights[:, 0][None, :, None, None]
    second = weights[:, 1][None, :, None, None]
    third = weights[:, 2][None, :, None, None]
    fourth = weights[:, 3][None, :, None, None]
    return first * colours[:, :, :-1, :-1] + second * colours[:, :, 1:, :-1] + third * colours[:, :, :-1, 1:] + fourth * colours[:, :, 1:, 1:]

def composite(samples):
    passing = jnp.cumprod(1.0 - samples[3], axis=0)
    before = jnp.concatenate([jnp.ones_like(passing[:1]), passing[:-1]], axis=0)
    return lax.optimization_barrier(jnp.sum(before[None] * samples, axis=1))

def neighbour(blocks, row_y, row_z):
    present = (row_y >= 0) & (row_y < GY) & (row_z >= 0) & (row_z < GZ)
    portion = blocks[:, jnp.clip(row_y, 0, GY - 1), jnp.clip(row_z, 0, GZ - 1)]
    return jnp.where(present, portion, jnp.zeros_like(portion))

def extended(blocks, brick_y, brick_z):
    layers = []
    for step_z in (-1, 0, 1):
        pieces = []
        for step_y in (-1, 0, 1):
            portion = neighbour(blocks, brick_y + step_y, brick_z + step_z)
            if step_y == -1:
                portion = portion[:, :, -1:, :]
            elif step_y == 1:
                portion = portion[:, :, :2, :]
            pieces.append(portion)
        column = jnp.concatenate(pieces, axis=2)
        if step_z == -1:
            column = column[..., -1:]
        elif step_z == 1:
            column = column[..., :2]
        layers.append(column)
    joined = jnp.concatenate(layers, axis=3)
    return joined.reshape(GX * CX, CY + 3, CZ + 3)

def reference(density, material, colour_table, opacity_table, centre_table, slice_weights, front_flags):
    dens_blocks = density.reshape(GX, GY, GZ, CX, CY, CZ)
    kind_blocks = material.reshape(GX, GY, GZ, CX, CY, CZ)
    weight_blocks = slice_weights.reshape(GX, GY, GZ, CX, 4)
    forward = front_flags[0, ROUNDS] == 1

    def render(column_id):
        brick_y = column_id // GZ
        brick_z = column_id % GZ
        values = extended(dens_blocks, brick_y, brick_z).astype(jnp.float32)
        materials = extended(kind_blocks, brick_y, brick_z)
        padded = jnp.pad(values, ((1, 1), (0, 0), (0, 0)))
        centred = values[:, 1:CY + 2, 1:CZ + 2]
        grad_x = (padded[2:, 1:CY + 2, 1:CZ + 2] - padded[:-2, 1:CY + 2, 1:CZ + 2]) * 0.5
        grad_y = (values[:, 2:, 1:CZ + 2] - values[:, :CY + 1, 1:CZ + 2]) * 0.5
        grad_z = (values[:, 1:CY + 2, 2:] - values[:, 1:CY + 2, :CZ + 1]) * 0.5
        colours = classify(centred, materials[:, 1:CY + 2, 1:CZ + 2], grad_x, grad_y, grad_z, colour_table, opacity_table, centre_table)
        inside_rows = (brick_y < GY - 1) | (jnp.arange(CY + 1) < CY)
        inside_cols = (brick_z < GZ - 1) | (jnp.arange(CZ + 1) < CZ)
        inside = inside_rows[:, None] & inside_cols[None, :]
        colours = jnp.where(inside[None, None], colours, jnp.zeros_like(colours))
        weights = weight_blocks[:, brick_y, brick_z].reshape(GX * CX, 4)
        weights = weights / lax.optimization_barrier(jnp.sum(weights, axis=1, keepdims=True))
        samples = resample(colours, weights)
        samples = jnp.where(forward, samples, jnp.flip(samples, axis=1))
        picture = composite(samples)
        return picture.reshape(4, GX, CY * CZ // GX)
    frames = lax.map(render, jnp.arange(GY * GZ))
    return jnp.transpose(frames, (1, 2, 0, 3)).reshape(4, BRICKS, CY * CZ // GX)
```

```python
import jax
import jax.numpy as jnp
from jax import lax
from jax.experimental import pallas as pl
from jax.experimental.pallas import tpu as pltpu
from jax.sharding import PartitionSpec as P

GX = 16
GY = 16
GZ = 2
MATS = 8
CX = 4
CY = 128
CZ = 256
SLAB = CY // 2
MESH = pl.DeviceIdType.MESH
SCALE = 2.0**20


def place(bx, by, bz):
    return ((bx * GY + by) * GZ + bz,)


def kernel(
    den, mat, col, opa, cen, wts, flg, out,
    dbuf, mbuf, wbuf, col_s, opa_s, cen_s, flg_s, wrep, tabs, qbuf, row_out, row_in, sbuf, rbuf,
    local_sems, core_send, core_recv, face_send, face_recv, edge_send, edge_recv,
    row_sems, part_send, part_recv,
):
    me = lax.axis_index("bricks")
    bx = me // (GY * GZ)
    by = (me // GZ) % GY
    c = me % GZ
    other = 1 - c

    own_rows = pl.multiple_of(c * 48, 16)
    own_dst = pl.multiple_of(other * 16, 16)
    own_mat = pl.multiple_of(c * SLAB, 16)
    locals_ = [
        pltpu.make_async_copy(
            den.at[0, :, pl.ds(own_rows, 80), :],
            dbuf.at[c, pl.ds(1, CX), pl.ds(own_dst, 80), :],
            local_sems.at[0],
        ),
        pltpu.make_async_copy(
            mat.at[0, :, pl.ds(own_mat, SLAB), :], mbuf.at[c], local_sems.at[1]
        ),
        pltpu.make_async_copy(wts.at[0], wbuf.at[c], local_sems.at[2]),
        pltpu.make_async_copy(col, col_s, local_sems.at[3]),
        pltpu.make_async_copy(opa, opa_s, local_sems.at[4]),
        pltpu.make_async_copy(cen, cen_s, local_sems.at[5]),
        pltpu.make_async_copy(flg, flg_s, local_sems.at[6]),
    ]
    for copy in locals_:
        copy.start()

    barrier = pltpu.get_barrier_semaphore()

    def tell(target):
        pl.semaphore_signal(barrier, inc=1, device_id=target, device_id_type=MESH)

    tell(place(bx, by, other))

    @pl.when(bx > 0)
    def _():
        tell(place(bx - 1, by, 0))
        tell(place(bx - 1, by, 1))

    @pl.when(bx < GX - 1)
    def _():
        tell(place(bx + 1, by, 0))
        tell(place(bx + 1, by, 1))

    @pl.when((c == 0) & (by > 0))
    def _():
        tell(place(bx, by - 1, 0))
        tell(place(bx, by - 1, 1))

    @pl.when((c == 1) & (by < GY - 1))
    def _():
        tell(place(bx, by + 1, 0))
        tell(place(bx, by + 1, 1))

    source_core = bx // 8
    keeps_own = source_core == c

    def tell_part(k, _):
        @pl.when(jnp.logical_not(keeps_own & (k == bx)))
        def _():
            tell(place(k, by, source_core))

        return 0

    lax.fori_loop(0, GX, tell_part, 0)

    @pl.when(bx == 0)
    def _():
        dbuf[:, 0] = jnp.zeros(dbuf.shape[:1] + dbuf.shape[2:], dbuf.dtype)

    @pl.when(bx == GX - 1)
    def _():
        dbuf[:, CX + 1] = jnp.zeros(dbuf.shape[:1] + dbuf.shape[2:], dbuf.dtype)

    @pl.when((c == 0) & (by == 0))
    def _():
        dbuf[:, 1 : CX + 1, 0:16, :] = jnp.zeros((GZ, CX, 16, CZ), dbuf.dtype)

    last_slab = (c == 1) & (by == GY - 1)

    @pl.when(last_slab)
    def _():
        dbuf[:, 1 : CX + 1, 80:96, :] = jnp.zeros((GZ, CX, 16, CZ), dbuf.dtype)
        row_in[...] = jnp.zeros(row_in.shape, row_in.dtype)

    peers = 16 + 2 * jnp.minimum(bx, 1) + 2 * jnp.minimum(GX - 1 - bx, 1)
    peers = peers + jnp.minimum(by, 1) + jnp.minimum(GY - 1 - by, 1)
    peers = peers + (source_core + c) % 2
    pl.semaphore_wait(barrier, peers)

    def remote(src, dst, send, recv, target):
        return pltpu.make_async_remote_copy(
            src_ref=src, dst_ref=dst, send_sem=send, recv_sem=recv,
            device_id=target, device_id_type=MESH,
        )

    up_faces = [
        remote(
            den.at[0, CX - 1, pl.ds(h * SLAB, SLAB), :],
            dbuf.at[c, 0, pl.ds(16, SLAB), :],
            face_send.at[h], face_recv.at[c], place(bx + 1, by, h),
        )
        for h in range(2)
    ]
    down_faces = [
        remote(
            den.at[0, 0, pl.ds(h * SLAB, SLAB), :],
            dbuf.at[c, CX + 1, pl.ds(16, SLAB), :],
            face_send.at[2 + h], face_recv.at[2 + c], place(bx - 1, by, h),
        )
        for h in range(2)
    ]

    @pl.when(bx < GX - 1)
    def _():
        for copy in up_faces:
            copy.start()

    @pl.when(bx > 0)
    def _():
        for copy in down_faces:
            copy.start()

    away_rows = pl.multiple_of(other * 48, 16)
    away_dst = pl.multiple_of(c * 16, 16)
    away_mat = pl.multiple_of(other * SLAB, 16)
    swaps = [
        remote(
            den.at[0, :, pl.ds(away_rows, 80), :],
            dbuf.at[c, pl.ds(1, CX), pl.ds(away_dst, 80), :],
            core_send.at[0], core_recv.at[0], place(bx, by, other),
        ),
        remote(
            mat.at[0, :, pl.ds(away_mat, SLAB), :], mbuf.at[c],
            core_send.at[1], core_recv.at[1], place(bx, by, other),
        ),
        remote(wts.at[0], wbuf.at[c], core_send.at[2], core_recv.at[2], place(bx, by, other)),
    ]
    for copy in swaps:
        copy.start()

    last_rows = remote(
        den.at[0, :, pl.ds(CY - 16, 16), :], dbuf.at[c, pl.ds(1, CX), pl.ds(0, 16), :],
        edge_send.at[0], edge_recv.at[c], place(bx, by + 1, 0),
    )
    first_rows = remote(
        den.at[0, :, pl.ds(0, 16), :], dbuf.at[c, pl.ds(1, CX), pl.ds(80, 16), :],
        edge_send.at[1], edge_recv.at[c], place(bx, by - 1, 1),
    )

    @pl.when(by < GY - 1)
    def _():
        last_rows.start()

    @pl.when(by > 0)
    def _():
        first_rows.start()

    for copy in locals_:
        copy.wait()

    rows8 = lax.broadcasted_iota(jnp.int32, (8, 128), 0)

    def spread(entry):
        full = jnp.zeros((8, 128), jnp.float32)
        for k in range(MATS):
            full = jnp.where(rows8 == k, entry(k), full)
        return full

    tabs[0] = spread(lambda k: opa_s[k])
    tabs[1] = spread(lambda k: cen_s[k])
    for ch in range(3):
        tabs[2 + ch] = spread(lambda k, ch=ch: col_s[ch, k])

    swaps[2].wait_recv()
    for b in range(GZ):
        weights = wbuf[b]
        weights = weights / jnp.sum(weights, axis=1, keepdims=True)
        for s in range(CX):
            for k in range(4):
                wrep[b, s * 4 + k] = jnp.broadcast_to(weights[s : s + 1, k : k + 1], (8, 128))

    swaps[0].wait_recv()
    swaps[1].wait_recv()

    @pl.when(((c == 0) & (by > 0)) | ((c == 1) & (by < GY - 1)))
    def _():
        for b in range(GZ):
            remote(
                den.at[0, :, pl.ds(0, 16), :], dbuf.at[b, pl.ds(1, CX), pl.ds(0, 16), :],
                edge_send.at[0], edge_recv.at[b], place(bx, by, other),
            ).wait_recv()

    def wait_face(which, b):
        remote(
            den.at[0, 0, pl.ds(0, SLAB), :], dbuf.at[b, 0, pl.ds(16, SLAB), :],
            face_send.at[0], face_recv.at[2 * which + b], place(bx, by, other),
        ).wait_recv()

    @pl.when(bx > 0)
    def _():
        for b in range(GZ):
            wait_face(0, b)

    @pl.when(bx < GX - 1)
    def _():
        for b in range(GZ):
            wait_face(1, b)

    lane512 = lax.broadcasted_iota(jnp.int32, (16, 2 * CZ), 1)
    row16 = lax.broadcasted_iota(jnp.int32, (16, 2 * CZ), 0)
    lane128 = lax.broadcasted_iota(jnp.int32, (8, 128), 1)

    def lookup(kinds):
        found = [[] for _ in range(5)]
        for r in range(2):
            parts = [[] for _ in range(5)]
            for lc in range(4):
                index = kinds[r * 8 : r * 8 + 8, lc * 128 : lc * 128 + 128]
                for t in range(5):
                    parts[t].append(jnp.take_along_axis(tabs[t], index, axis=0))
            for t in range(5):
                found[t].append(jnp.concatenate(parts[t], axis=1))
        return [jnp.concatenate(f, axis=0) for f in found]

    def shade(p):
        base = pl.multiple_of(16 * p, 16)

        def load(sl, start):
            halves = [dbuf[b, sl, pl.ds(start, 16), :] for b in range(GZ)]
            return jnp.concatenate(halves, axis=1).astype(jnp.float32)

        for s in range(CX):
            here = load(s + 1, base + 16)
            above = load(s + 1, base)
            below = load(s + 1, base + 32)
            gx = load(s + 2, base + 16) - load(s, base + 16)
            up = jnp.where(row16 == 15, pltpu.roll(below, 15, 0), pltpu.roll(here, 15, 0))
            down = jnp.where(row16 == 0, pltpu.roll(above, 1, 0), pltpu.roll(here, 1, 0))
            gy = up - down
            right = jnp.where(lane512 == 2 * CZ - 1, 0.0, pltpu.roll(here, 2 * CZ - 1, 1))
            left = jnp.where(lane512 == 0, 0.0, pltpu.roll(here, 1, 1))
            gz = right - left
            kinds = jnp.concatenate([mbuf[b, s, pl.ds(base, 16), :] for b in range(GZ)], axis=1)
            opacity, centre, red, green, blue = lookup(kinds)
            absorb = opacity / (1.0 + jnp.exp(2.0 * (centre - here)))
            squares = gx * gx + gy * gy + gz * gz
            facing = jnp.abs(0.3 * gx + 0.24 * gy + 0.32 * gz) * lax.rsqrt(0.25 * squares + 1.0)
            weight = (0.35 + 0.65 * facing) * absorb
            for ch, value in enumerate((red * weight, green * weight, blue * weight, absorb)):
                qbuf[s * 4 + ch, pl.ds(base, 16), :] = value

    shade(0)
    for k in range(16):
        row_out[k : k + 1, :] = qbuf[k, 0:1, :]

    row_target = jnp.where(c == 1, me - 1, me - 2 * 1 + 1)
    row_copy = remote(row_out, row_in, row_sems.at[0], row_sems.at[1], (row_target,))
    has_previous = (c == 1) | (by > 0)

    @pl.when(has_previous)
    def _():
        row_copy.start()

    def shade_step(p, _):
        shade(p)
        return 0

    lax.fori_loop(1, 4, shade_step, 0)

    @pl.when(jnp.logical_not(last_slab))
    def _():
        row_copy.wait_recv()

    for k in range(16):
        qbuf[k, SLAB : SLAB + 1, :] = row_in[k : k + 1, :]

    forward = flg_s[0, 4]
    j0 = bx % 8

    def group(i, _):
        j = (j0 + i) % 8
        base = pl.multiple_of(8 * j, 8)
        total = [[None] * 4 for _ in range(4)]
        passing = [None] * 4
        for order in range(CX):
            s = order * forward + (CX - 1 - order) * (1 - forward)
            for ch in (3, 0, 1, 2):
                now = [qbuf[s * 4 + ch, pl.ds(base, 8), pl.ds(lc * 128, 128)] for lc in range(4)]
                nxt = [
                    jnp.where(
                        rows8 == 7,
                        qbuf[s * 4 + ch, pl.ds(base + 8, 1), pl.ds(lc * 128, 128)],
                        pltpu.roll(now[lc], 7, 0),
                    )
                    for lc in range(4)
                ]
                w = [[wrep[b, s * 4 + k] for k in range(4)] for b in range(GZ)]
                near, far = [], []
                for lc in range(4):
                    b = lc // 2
                    near.append(w[b][0] * now[lc] + w[b][1] * nxt[lc])
                    far.append(pltpu.roll(w[b][2] * now[lc] + w[b][3] * nxt[lc], 127, 1))
                cross = pltpu.roll(w[0][2] * now[2] + w[0][3] * nxt[2], 127, 1)
                following = [far[1], cross, far[3], jnp.zeros((8, 128), jnp.float32)]
                for lc in range(4):
                    sample = near[lc] + jnp.where(lane128 == 127, following[lc], far[lc])
                    if ch == 3:
                        before = passing[lc]
                        passing[lc] = 1.0 - sample if before is None else before * (1.0 - sample)
                        held = before
                        if lc == 0:
                            befores = []
                        befores.append(held)
                    if befores[lc] is None:
                        total[ch][lc] = sample
                    else:
                        total[ch][lc] = total[ch][lc] + befores[lc] * sample
        for b in range(GZ):
            for pair in range(2):
                halves = []
                for ch in (2 * pair, 2 * pair + 1):
                    wide = jnp.concatenate([total[ch][2 * b], total[ch][2 * b + 1]], axis=1)
                    wide = wide * SCALE
                    wide = wide * wide
                    halves.append(wide * wide)
                sbuf[j, b, pl.ds(16 * pair, 16), :] = jnp.concatenate(halves, axis=0).astype(
                    jnp.bfloat16
                )
        target_x = 8 * c + j
        for b in range(GZ):
            mine = (target_x == bx) & (c == b)

            @pl.when(mine)
            def _(b=b):
                pltpu.make_async_copy(sbuf.at[j, b], rbuf.at[bx], local_sems.at[7]).start()

            @pl.when(jnp.logical_not(mine))
            def _(b=b):
                remote(
                    sbuf.at[j, b], rbuf.at[bx], part_send.at[j, b], part_recv.at[bx],
                    place(target_x, by, b),
                ).start()

        return 0

    lax.fori_loop(0, 8, group, 0)

    def take(k, _):
        own = keeps_own & (k == bx)

        @pl.when(own)
        def _():
            pltpu.make_async_copy(sbuf.at[0, 0], rbuf.at[k], local_sems.at[7]).wait()

        @pl.when(jnp.logical_not(own))
        def _():
            remote(
                sbuf.at[0, 0], rbuf.at[k], part_send.at[0, 0], part_recv.at[k], place(bx, by, other)
            ).wait_recv()

        return 0

    lax.fori_loop(0, GX, take, 0)

    def decode(values):
        return lax.rsqrt(lax.rsqrt(values.astype(jnp.float32)))

    def part(order):
        k = order * forward + (GX - 1 - order) * (1 - forward)
        return decode(rbuf[k]) * (1.0 / SCALE)

    first = part(0)
    acc = [first[8 * ch : 8 * ch + 8] for ch in range(4)]
    clear = 1.0 - acc[3]
    for order in range(1, GX):
        nxt = part(order)
        pieces = [nxt[8 * ch : 8 * ch + 8] for ch in range(4)]
        for ch in range(4):
            acc[ch] = acc[ch] + clear * pieces[ch]
        clear = clear * (1.0 - pieces[3])
    for ch in range(4):
        for lc in range(2):
            out[ch, pl.ds(lc, 8, 2), :] = acc[ch][:, lc * 128 : lc * 128 + 128]

    @pl.when(bx < GX - 1)
    def _():
        for copy in up_faces:
            copy.wait_send()

    @pl.when(bx > 0)
    def _():
        for copy in down_faces:
            copy.wait_send()

    for copy in swaps:
        copy.wait_send()

    @pl.when(by < GY - 1)
    def _():
        last_rows.wait_send()

    @pl.when(by > 0)
    def _():
        first_rows.wait_send()

    @pl.when(has_previous)
    def _():
        row_copy.wait_send()

    def sent(j, _):
        for b in range(GZ):

            @pl.when(jnp.logical_not((8 * c + j == bx) & (c == b)))
            def _(b=b):
                remote(
                    sbuf.at[j, b], rbuf.at[bx], part_send.at[j, b], part_recv.at[bx],
                    place(bx, by, other),
                ).wait_send()

        return 0

    lax.fori_loop(0, 8, sent, 0)


def body(density, material, colour_table, opacity_table, centre_table, slice_weights, front_flags):
    any_space = pl.BlockSpec(memory_space=pltpu.HBM)
    frame = pl.pallas_call(
        kernel,
        out_shape=jax.ShapeDtypeStruct((4, 16, 128), jnp.float32),
        in_specs=[any_space] * 7,
        out_specs=pl.BlockSpec(memory_space=pltpu.VMEM),
        scratch_shapes=[
            pltpu.VMEM((GZ, CX + 2, SLAB + 32, CZ), jnp.bfloat16),
            pltpu.VMEM((GZ, CX, SLAB, CZ), jnp.int32),
            pltpu.VMEM((GZ, CX, 4), jnp.float32),
            pltpu.SMEM((3, MATS), jnp.float32),
            pltpu.SMEM((MATS,), jnp.float32),
            pltpu.SMEM((MATS,), jnp.float32),
            pltpu.SMEM((1, 5), jnp.int32),
            pltpu.VMEM((GZ, 16, 8, 128), jnp.float32),
            pltpu.VMEM((5, 8, 128), jnp.float32),
            pltpu.VMEM((16, SLAB + 8, 2 * CZ), jnp.float32),
            pltpu.VMEM((16, 2 * CZ), jnp.float32),
            pltpu.VMEM((16, 2 * CZ), jnp.float32),
            pltpu.VMEM((8, GZ, 32, CZ), jnp.bfloat16),
            pltpu.VMEM((GX, 32, CZ), jnp.bfloat16),
            pltpu.SemaphoreType.DMA((8,)),
            pltpu.SemaphoreType.DMA((3,)),
            pltpu.SemaphoreType.DMA((3,)),
            pltpu.SemaphoreType.DMA((4,)),
            pltpu.SemaphoreType.DMA((4,)),
            pltpu.SemaphoreType.DMA((2,)),
            pltpu.SemaphoreType.DMA((2,)),
            pltpu.SemaphoreType.DMA((2,)),
            pltpu.SemaphoreType.DMA((8, GZ)),
            pltpu.SemaphoreType.DMA((GX,)),
        ],
        compiler_params=pltpu.CompilerParams(
            collective_id=0, has_side_effects=True, vmem_limit_bytes=64 * 2**20 - 2**16
        ),
    )(
        density, material, colour_table.T, opacity_table, centre_table, slice_weights, front_flags
    )
    return frame.reshape(4, 1, 2048)


def solution(mesh):
    in_specs = (
        P("bricks", None, None, None),
        P("bricks", None, None, None),
        P(),
        P(),
        P(),
        P("bricks", None, None),
        P("bricks", None),
    )
    out_specs = P(None, "bricks", None)
    return jax.shard_map(body, mesh=mesh, in_specs=in_specs, out_specs=out_specs, check_vma=False)
```

```python
import jax
import jax.numpy as jnp
from jax import lax
from jax.experimental import pallas as pl
from jax.experimental.pallas import tpu as pltpu
from jax.sharding import PartitionSpec as P

GX = 16
GY = 16
GZ = 2
MATS = 8
CX = 4
CY = 128
CZ = 256
SLAB = CY // 2
MESH = pl.DeviceIdType.MESH
SCALE = 2.0**20
LOG2E = 1.4426950408889634


def place(bx, by, bz):
    return ((bx * GY + by) * GZ + bz,)


def kernel(
    den, mat, col, opa, cen, wts, flg, out,
    dbuf, mbuf, wbuf, col_s, opa_s, cen_s, flg_s, wrep, tabs, qbuf, held, mids, sbuf, rbuf,
    local_sems, core_send, core_recv, face_send, face_recv, edge_send, edge_recv,
    kind_recv, corner_recv, part_send, part_recv, relay, late,
):
    me = lax.axis_index("bricks")
    bx = me // (GY * GZ)
    by = (me // GZ) % GY
    c = me % GZ
    other = 1 - c

    barrier = pltpu.get_barrier_semaphore()

    def tell(target):
        pl.semaphore_signal(barrier, inc=1, device_id=target, device_id_type=MESH)

    source_core = bx // 8
    keeps_own = source_core == c
    column = bx % 4
    level = bx // 4
    ring = [
        level * 4 + (column + 1) % 4,
        level * 4 + (column + 3) % 4,
        ((level + 1) % 4) * 4 + column,
        ((level + 3) % 4) * 4 + column,
    ]
    @pl.when((c == 0) & (by > 0))
    def _():
        tell(place(bx, by - 1, 0))
        tell(place(bx, by - 1, 1))

    @pl.when((c == 1) & (by < GY - 1))
    def _():
        tell(place(bx, by + 1, 0))
        tell(place(bx, by + 1, 1))

        @pl.when(bx > 0)
        def _():
            tell(place(bx - 1, by + 1, 0))
            tell(place(bx - 1, by + 1, 1))

        @pl.when(bx < GX - 1)
        def _():
            tell(place(bx + 1, by + 1, 0))
            tell(place(bx + 1, by + 1, 1))

    latest = me == 0
    near_latest = (by == 0) & ((me == 1) | (bx == 1))

    @pl.when(jnp.logical_not(latest))
    def _():
        tell(place(bx, by, other))
        for near in ring:
            tell(place(near, by, 0))
            tell(place(near, by, 1))

    beside = (bx == 1) | (bx == 3) | (bx == 4) | (bx == 12)

    @pl.when((by == 0) & (bx > 0) & jnp.logical_not(beside))
    def _():
        tell(place(0, 0, 0))

    diagonals = [
        ((level + dy) % 4) * 4 + (column + dx) % 4 for dx in (1, 3) for dy in (1, 3)
    ]
    wraps_up = (column == 3) & (bx < GX - 1)
    wraps_down = (column == 0) & (bx > 0)

    @pl.when(wraps_up)
    def _():
        tell(place(bx + 1, by, 0))
        tell(place(bx + 1, by, 1))

    @pl.when(wraps_down)
    def _():
        tell(place(bx - 1, by, 0))
        tell(place(bx - 1, by, 1))

    own_rows = pl.multiple_of(c * 48, 16)
    own_dst = pl.multiple_of(other * 16, 16)
    own_mat = pl.multiple_of(c * 56, 8)
    own_mat_dst = pl.multiple_of(other * 8, 8)
    locals_ = [
        pltpu.make_async_copy(
            den.at[0, :, pl.ds(own_rows, 80), :],
            dbuf.at[c, pl.ds(1, CX), pl.ds(own_dst, 80), :],
            local_sems.at[0],
        ),
        pltpu.make_async_copy(
            mat.at[0, :, pl.ds(own_mat, 72), :],
            mbuf.at[c, :, pl.ds(own_mat_dst, 72), :],
            local_sems.at[1],
        ),
        pltpu.make_async_copy(wts.at[0], wbuf.at[c], local_sems.at[2]),
        pltpu.make_async_copy(col, col_s, local_sems.at[3]),
        pltpu.make_async_copy(opa, opa_s, local_sems.at[4]),
        pltpu.make_async_copy(cen, cen_s, local_sems.at[5]),
        pltpu.make_async_copy(flg, flg_s, local_sems.at[6]),
    ]
    for copy in locals_:
        copy.start()

    @pl.when(bx == 0)
    def _():
        dbuf[:, 0] = jnp.zeros(dbuf.shape[:1] + dbuf.shape[2:], dbuf.dtype)

    @pl.when(bx == GX - 1)
    def _():
        dbuf[:, CX + 1] = jnp.zeros(dbuf.shape[:1] + dbuf.shape[2:], dbuf.dtype)

    @pl.when((c == 0) & (by == 0))
    def _():
        dbuf[:, 1 : CX + 1, 0:16, :] = jnp.zeros((GZ, CX, 16, CZ), dbuf.dtype)

    last_slab = (c == 1) & (by == GY - 1)

    @pl.when(last_slab)
    def _():
        dbuf[:, 1 : CX + 1, 80:96, :] = jnp.zeros((GZ, CX, 16, CZ), dbuf.dtype)
        qbuf[:, SLAB:, :] = jnp.zeros((16, 8, 2 * CZ), jnp.float32)

    peers = 9 + jnp.minimum(by, 1) + jnp.minimum(GY - 1 - by, 1)
    peers = peers + 2 * (column // 3) * jnp.minimum(GX - 1 - bx, 1)
    peers = peers + 2 * ((3 - column) // 3) * jnp.minimum(bx, 1)
    peers = peers + jnp.minimum(by, 1) * (jnp.minimum(bx, 1) + jnp.minimum(GX - 1 - bx, 1))
    first = 1 - jnp.minimum(by, 1)
    ringed = 1 - jnp.minimum((bx - 1) * (bx - 1) * (bx - 3) * (bx - 3), 1)
    ringed = ringed + 1 - jnp.minimum((bx - 4) * (bx - 4) * (bx - 12) * (bx - 12), 1)
    sibling = c * (1 - jnp.minimum(bx, 1))
    peers = peers - first * (ringed + sibling)
    peers = peers + 22 * (1 - jnp.minimum(me, 1))
    pl.semaphore_wait(barrier, peers)

    def announce(target):
        pl.semaphore_signal(late, inc=1, device_id=target, device_id_type=MESH)

    @pl.when(latest)
    def _():
        announce(place(0, 0, 1))
        announce(place(1, 0, 0))
        announce(place(1, 0, 1))

    def remote(src, dst, send, recv, target):
        return pltpu.make_async_remote_copy(
            src_ref=src, dst_ref=dst, send_sem=send, recv_sem=recv,
            device_id=target, device_id_type=MESH,
        )

    away_rows = pl.multiple_of(other * 48, 16)
    away_dst = pl.multiple_of(c * 16, 16)
    away_mat = pl.multiple_of(other * 56, 8)
    away_mat_dst = pl.multiple_of(c * 8, 8)
    swaps = [
        remote(
            den.at[0, :, pl.ds(away_rows, 80), :],
            dbuf.at[c, pl.ds(1, CX), pl.ds(away_dst, 80), :],
            core_send.at[0], core_recv.at[0], place(bx, by, other),
        ),
        remote(
            mat.at[0, :, pl.ds(away_mat, 72), :], mbuf.at[c, :, pl.ds(away_mat_dst, 72), :],
            core_send.at[1], core_recv.at[1], place(bx, by, other),
        ),
        remote(wts.at[0], wbuf.at[c], core_send.at[2], core_recv.at[2], place(bx, by, other)),
    ]
    @pl.when(me != 1)
    def _():
        for copy in swaps:
            copy.start()

    up_faces = [
        remote(
            den.at[0, CX - 1, pl.ds(h * SLAB, 80 - 16 * h), :],
            dbuf.at[c, 0, pl.ds(16, 80 - 16 * h), :],
            face_send.at[h], face_recv.at[c], place(bx + 1, by, h),
        )
        for h in range(2)
    ]
    down_faces = [
        remote(
            den.at[0, 0, pl.ds(h * SLAB, 80 - 16 * h), :],
            dbuf.at[c, CX + 1, pl.ds(16, 80 - 16 * h), :],
            face_send.at[2 + h], face_recv.at[2 + c], place(bx - 1, by, h),
        )
        for h in range(2)
    ]

    @pl.when(bx < GX - 1)
    def _():
        for copy in up_faces:
            copy.start()

    @pl.when(bx > 0)
    def _():
        down_faces[1].start()

        @pl.when(jnp.logical_not(near_latest))
        def _():
            down_faces[0].start()

    last_rows = remote(
        den.at[0, :, pl.ds(CY - 16, 16), :], dbuf.at[c, pl.ds(1, CX), pl.ds(0, 16), :],
        edge_send.at[0], edge_recv.at[c], place(bx, by + 1, 0),
    )
    first_rows = remote(
        den.at[0, :, pl.ds(0, 16), :], dbuf.at[c, pl.ds(1, CX), pl.ds(80, 16), :],
        edge_send.at[1], edge_recv.at[c], place(bx, by - 1, 1),
    )

    first_kinds = remote(
        mat.at[0, :, pl.ds(0, 8), :], mbuf.at[c, :, pl.ds(72, 8), :],
        edge_send.at[2], kind_recv.at[c], place(bx, by - 1, 1),
    )
    up_corner = remote(
        den.at[0, CX - 1, pl.ds(0, 16), :], dbuf.at[c, 0, pl.ds(80, 16), :],
        edge_send.at[3], corner_recv.at[c], place(bx + 1, by - 1, 1),
    )
    down_corner = remote(
        den.at[0, 0, pl.ds(0, 16), :], dbuf.at[c, CX + 1, pl.ds(80, 16), :],
        edge_send.at[4], corner_recv.at[2 + c], place(bx - 1, by - 1, 1),
    )

    @pl.when(by < GY - 1)
    def _():
        last_rows.start()

    @pl.when(by > 0)
    def _():
        first_rows.start()

        @pl.when(bx < GX - 1)
        def _():
            up_corner.start()

        @pl.when(bx > 0)
        def _():
            down_corner.start()

        first_kinds.start()

    def pass_on(step, chips):
        @pl.when(jnp.logical_not(latest))
        def _():
            for near in chips:

                @pl.when((near * GY + by + c) != 0)
                def _(near=near):
                    pl.semaphore_signal(
                        relay.at[step], inc=1, device_id=place(near, by, c), device_id_type=MESH
                    )

        @pl.when(me == 1)
        def _():
            for near in chips:
                pl.semaphore_signal(
                    relay.at[step], inc=1, device_id=place(near, by, 0), device_id_type=MESH
                )

    def hear(step):
        @pl.when(jnp.logical_not(latest))
        def _():
            pl.semaphore_wait(relay.at[step], 4)

    @pl.when(latest)
    def _():
        for k in range(2, GX):
            announce(place(k, 0, 0))

    pass_on(0, ring)
    for copy in locals_:
        copy.wait()

    rows8 = lax.broadcasted_iota(jnp.int32, (8, 128), 0)

    def spread(entry):
        full = jnp.zeros((8, 128), jnp.float32)
        for k in range(MATS):
            full = jnp.where(rows8 == k, entry(k), full)
        return full

    tabs[0] = spread(lambda k: opa_s[k])
    tabs[1] = spread(lambda k: cen_s[k]) * (2.0 * LOG2E)
    for ch in range(3):
        tabs[2 + ch] = spread(lambda k, ch=ch: col_s[ch, k])

    hear(0)
    pass_on(1, diagonals)

    @pl.when(near_latest)
    def _():
        pl.semaphore_wait(late, 1)

        @pl.when(me == 1)
        def _():
            for copy in swaps:
                copy.start()

        @pl.when(me != 1)
        def _():
            down_faces[0].start()

    swaps[2].wait_recv()
    for b in range(GZ):
        weights = wbuf[b]
        weights = weights / jnp.sum(weights, axis=1, keepdims=True)
        for s in range(CX):
            for k in range(4):
                wrep[b, s * 4 + k] = jnp.broadcast_to(weights[s : s + 1, k : k + 1], (8, 128))

    swaps[0].wait_recv()
    swaps[1].wait_recv()

    rows512 = lax.broadcasted_iota(jnp.int32, (8, 2 * CZ), 0)
    lane128 = lax.broadcasted_iota(jnp.int32, (8, 128), 1)

    def shade(p, rows=16):
        base = pl.multiple_of(16 * p, 16)
        mat_base = pl.multiple_of(16 * p + 8, 8)

        def load(sl, start):
            halves = [dbuf[b, sl, pl.ds(start, 16), :] for b in range(GZ)]
            return jnp.concatenate(halves, axis=1).astype(jnp.float32)

        for s in range(CX):
            block = load(s + 1, base + 16)
            parts = [load(s + 1, base)[8:], block[:8], block[8:]]
            if rows == 16:
                parts.append(load(s + 1, base + 32)[:8])
            for r in range(rows // 8):
                at = pl.multiple_of(base + 8 * r, 8)
                here = parts[r + 1]
                up = jnp.where(
                    rows512 == 7, pltpu.roll(parts[r + 2], 7, 0), pltpu.roll(here, 7, 0)
                )
                down = jnp.where(
                    rows512 == 0, pltpu.roll(parts[r], 1, 0), pltpu.roll(here, 1, 0)
                )
                gy = up - down
                right = pltpu.roll(here, 2 * CZ - 1, 1)
                left = pltpu.roll(here, 1, 1)
                gz = jnp.concatenate(
                    [
                        right[:, :128] - jnp.where(lane128 == 0, 0.0, left[:, :128]),
                        right[:, 128:384] - left[:, 128:384],
                        jnp.where(lane128 == 127, 0.0, right[:, 384:]) - left[:, 384:],
                    ],
                    axis=1,
                )
                along = 0.24 * gy + 0.32 * gz
                squares = 0.25 * (gy * gy + gz * gz) + 1.0
                kinds = jnp.concatenate(
                    [
                        mbuf[b, s, pl.ds(pl.multiple_of(mat_base + 8 * r, 8), 8), :]
                        for b in range(GZ)
                    ],
                    axis=1,
                )

                def look(t):
                    return jnp.concatenate(
                        [
                            jnp.take_along_axis(
                                tabs[t], kinds[:, lc * 128 : lc * 128 + 128], axis=0
                            )
                            for lc in range(4)
                        ],
                        axis=1,
                    )

                below_one = 1.0 + jnp.exp2(look(1) - (2.0 * LOG2E) * here)
                inverse = pl.reciprocal(below_one, approx=True)
                absorb = look(0) * (inverse * (2.0 - below_one * inverse))
                weight = absorb
                if s in (1, 2):
                    gx = [
                        dbuf[b, s + 2, pl.ds(base + 16, 16), :].astype(jnp.float32)[8 * r : 8 * r + 8]
                        - dbuf[b, s, pl.ds(base + 16, 16), :].astype(jnp.float32)[8 * r : 8 * r + 8]
                        for b in range(GZ)
                    ]
                    gx = jnp.concatenate(gx, axis=1)
                    facing = jnp.abs(0.3 * gx + along) * lax.rsqrt(0.25 * (gx * gx) + squares)
                    weight = (0.35 + 0.65 * facing) * absorb
                else:
                    held[s // 3, 0, pl.ds(at, 8), :] = along
                    held[s // 3, 1, pl.ds(at, 8), :] = squares
                for ch in range(3):
                    qbuf[s * 4 + ch, pl.ds(at, 8), :] = look(2 + ch) * weight
                qbuf[s * 4 + 3, pl.ds(at, 8), :] = absorb

    def face_shade(p, rows=16):
        base = pl.multiple_of(16 * p, 16)

        def load(sl):
            halves = [dbuf[b, sl, pl.ds(base + 16, 16), :] for b in range(GZ)]
            return jnp.concatenate(halves, axis=1).astype(jnp.float32)[:rows]

        for s in (0, 3):
            gx = load(s + 2) - load(s)
            along = held[s // 3, 0, pl.ds(base, rows), :]
            squares = held[s // 3, 1, pl.ds(base, rows), :]
            facing = jnp.abs(0.3 * gx + along) * lax.rsqrt(0.25 * (gx * gx) + squares)
            factor = 0.35 + 0.65 * facing
            for ch in range(3):
                qbuf[s * 4 + ch, pl.ds(base, rows), :] = (
                    qbuf[s * 4 + ch, pl.ds(base, rows), :] * factor
                )

    forward = flg_s[0, 4]

    def slice_at(order):
        return order * forward + (CX - 1 - order) * (1 - forward)

    def resample(s, ch, base):
        now = [qbuf[s * 4 + ch, pl.ds(base, 8), pl.ds(lc * 128, 128)] for lc in range(4)]
        nxt = [
            jnp.where(
                rows8 == 7,
                qbuf[s * 4 + ch, pl.ds(base + 8, 1), pl.ds(lc * 128, 128)],
                pltpu.roll(now[lc], 7, 0),
            )
            for lc in range(4)
        ]
        w = [[wrep[b, s * 4 + k] for k in range(4)] for b in range(GZ)]
        near, far = [], []
        for lc in range(4):
            b = lc // 2
            near.append(w[b][0] * now[lc] + w[b][1] * nxt[lc])
            far.append(pltpu.roll(w[b][2] * now[lc] + w[b][3] * nxt[lc], 127, 1))
        cross = pltpu.roll(w[0][2] * now[2] + w[0][3] * nxt[2], 127, 1)
        following = [far[1], cross, far[3], jnp.zeros((8, 128), jnp.float32)]
        return [near[lc] + jnp.where(lane128 == 127, following[lc], far[lc]) for lc in range(4)]

    def middle(j):
        base = pl.multiple_of(8 * j, 8)
        opaque = [resample(slice_at(order), 3, base) for order in range(CX)]
        clear = [None, [], [], []]
        for lc in range(4):
            clear[1].append(1.0 - opaque[0][lc])
            clear[2].append(clear[1][lc] * (1.0 - opaque[1][lc]))
            clear[3].append(clear[2][lc] * (1.0 - opaque[2][lc]))
        for lc in range(4):
            lanes = pl.ds(lc * 128, 128)
            total = opaque[0][lc]
            for order in range(1, CX):
                total = total + clear[order][lc] * opaque[order][lc]
            mids[3, pl.ds(base, 8), lanes] = total
            mids[4, pl.ds(base, 8), lanes] = clear[3][lc]
        for ch in range(3):
            first = resample(slice_at(1), ch, base)
            second = resample(slice_at(2), ch, base)
            for lc in range(4):
                mids[ch, pl.ds(base, 8), pl.ds(lc * 128, 128)] = (
                    clear[1][lc] * first[lc] + clear[2][lc] * second[lc]
                )

    def middle_step(j, _):
        middle(j)
        return 0

    def shade_step(p, _):
        shade(p)
        return 0

    lax.fori_loop(1 - c, 4 - c, shade_step, 0)

    @pl.when(c == 0)
    def _():
        shade(4, 8)

    lax.fori_loop(2 - 2 * c, 8 - 3 * c, middle_step, 0)
    @pl.when(((c == 0) & (by > 0)) | ((c == 1) & (by < GY - 1)))
    def _():
        for b in range(GZ):
            remote(
                den.at[0, :, pl.ds(0, 16), :], dbuf.at[b, pl.ds(1, CX), pl.ds(0, 16), :],
                edge_send.at[0], edge_recv.at[b], place(bx, by, other),
            ).wait_recv()

    @pl.when((c == 1) & (by < GY - 1))
    def _():
        for b in range(GZ):
            remote(
                mat.at[0, :, pl.ds(0, 8), :], mbuf.at[b, :, pl.ds(72, 8), :],
                edge_send.at[2], kind_recv.at[b], place(bx, by, other),
            ).wait_recv()

    shade(3 * c)

    @pl.when((c == 1) & jnp.logical_not(last_slab))
    def _():
        shade(4, 8)

    lax.fori_loop(5 * c, 2 + 6 * c, middle_step, 0)

    def wait_face(which, b, rows):
        remote(
            den.at[0, 0, pl.ds(0, rows), :],
            dbuf.at[b, (CX + 1) * which, pl.ds(16, rows), :],
            face_send.at[0], face_recv.at[2 * which + b], place(bx, by, other),
        ).wait_recv()

    def wait_faces(which):
        for b in range(GZ):

            @pl.when(c == 1)
            def _(b=b):
                wait_face(which, b, SLAB)

            @pl.when(c == 0)
            def _(b=b):
                wait_face(which, b, 80)

    def wait_corners(which):
        for b in range(GZ):
            remote(
                den.at[0, 0, pl.ds(0, 16), :],
                dbuf.at[b, (CX + 1) * which, pl.ds(80, 16), :],
                face_send.at[0], corner_recv.at[2 * which + b], place(bx, by, other),
            ).wait_recv()

    @pl.when(bx > 0)
    def _():
        wait_faces(0)

    @pl.when(bx < GX - 1)
    def _():
        wait_faces(1)

    def face_step(p, _):
        face_shade(p)
        return 0

    same_half = 1 - (level // 2 + c) % 2
    far_level = (level + same_half) % 2

    def group(i, _):
        k = i % 4
        across = (2 - k) * (1 - k // 2) + (9 - 3 * k) * (k // 2)
        j = 4 * ((far_level + i // 4) % 2) + (column + across) % 4

        half = (far_level + i // 4) % 2
        later = i // 4

        @pl.when(k == 0)
        def _():
            lax.fori_loop(
                2 * half + later * half, 3 + half - later * (1 - half), face_step, 0
            )

        @pl.when((j == 7) & (c == 1) & (by < GY - 1))
        def _():
            @pl.when(bx > 0)
            def _():
                wait_corners(0)

            @pl.when(bx < GX - 1)
            def _():
                wait_corners(1)

        @pl.when((j == 7) & jnp.logical_not(last_slab))
        def _():
            face_shade(4, 8)

        base = pl.multiple_of(8 * j, 8)
        total = []
        for ch in range(3):
            first = resample(slice_at(0), ch, base)
            last = resample(slice_at(3), ch, base)
            total.append([
                first[lc]
                + mids[ch, pl.ds(base, 8), pl.ds(lc * 128, 128)]
                + mids[4, pl.ds(base, 8), pl.ds(lc * 128, 128)] * last[lc]
                for lc in range(4)
            ])
        total.append([mids[3, pl.ds(base, 8), pl.ds(lc * 128, 128)] for lc in range(4)])
        for b in range(GZ):
            for pair in range(2):
                halves = []
                for ch in (2 * pair, 2 * pair + 1):
                    wide = jnp.concatenate([total[ch][2 * b], total[ch][2 * b + 1]], axis=1)
                    wide = wide * SCALE
                    wide = wide * wide
                    halves.append(wide * wide)
                sbuf[2 * j + b, pl.ds(16 * pair, 16), :] = jnp.concatenate(halves, axis=0).astype(
                    jnp.bfloat16
                )

        @pl.when(i == 0)
        def _():
            hear(1)

        target_x = 8 * c + j

        for b in range(GZ):
            mine = (target_x == bx) & (c == b)

            @pl.when(mine)
            def _(b=b):
                pltpu.make_async_copy(sbuf.at[2 * j + b], rbuf.at[bx], part_recv).start()

            @pl.when(jnp.logical_not(mine) & (target_x + by + c + b > 0))
            def _(b=b):
                remote(
                    sbuf.at[2 * j + b], rbuf.at[bx], part_send, part_recv,
                    place(target_x, by, b),
                ).start()

        return 0

    lax.fori_loop(0, 8, group, 0)

    @pl.when((by + c == 0) & (bx > 0))
    def _():
        @pl.when(bx > 1)
        def _():
            pl.semaphore_wait(late, 1)

        remote(sbuf.at[0], rbuf.at[bx], part_send, part_recv, place(0, 0, 0)).start()

    remote(sbuf, rbuf, part_send, part_recv, place(bx, by, other)).wait_recv()

    def decode(values):
        return lax.rsqrt(lax.rsqrt(values.astype(jnp.float32)))

    def part(order):
        k = order * forward + (GX - 1 - order) * (1 - forward)
        return decode(rbuf[k]) * (1.0 / SCALE)

    first = part(0)
    acc = [first[8 * ch : 8 * ch + 8] for ch in range(4)]
    clear = 1.0 - acc[3]
    for order in range(1, GX):
        nxt = part(order)
        pieces = [nxt[8 * ch : 8 * ch + 8] for ch in range(4)]
        for ch in range(4):
            acc[ch] = acc[ch] + clear * pieces[ch]
        clear = clear * (1.0 - pieces[3])
    for ch in range(4):
        for lc in range(2):
            out[ch, pl.ds(lc, 8, 2), :] = acc[ch][:, lc * 128 : lc * 128 + 128]

    @pl.when(bx < GX - 1)
    def _():
        for copy in up_faces:
            copy.wait_send()

    @pl.when(bx > 0)
    def _():
        for copy in down_faces:
            copy.wait_send()

    for copy in swaps:
        copy.wait_send()

    @pl.when(by < GY - 1)
    def _():
        last_rows.wait_send()

    @pl.when(by > 0)
    def _():
        first_rows.wait_send()
        first_kinds.wait_send()

        @pl.when(bx < GX - 1)
        def _():
            up_corner.wait_send()

        @pl.when(bx > 0)
        def _():
            down_corner.wait_send()

    @pl.when(keeps_own)
    def _():
        remote(
            sbuf.at[pl.ds(0, 15)], rbuf.at[pl.ds(0, 15)], part_send, part_recv,
            place(bx, by, other),
        ).wait_send()

    @pl.when(jnp.logical_not(keeps_own))
    def _():
        remote(sbuf, rbuf, part_send, part_recv, place(bx, by, other)).wait_send()


def body(density, material, colour_table, opacity_table, centre_table, slice_weights, front_flags):
    any_space = pl.BlockSpec(memory_space=pltpu.HBM)
    frame = pl.pallas_call(
        kernel,
        out_shape=jax.ShapeDtypeStruct((4, 16, 128), jnp.float32),
        in_specs=[any_space] * 7,
        out_specs=pl.BlockSpec(memory_space=pltpu.VMEM),
        scratch_shapes=[
            pltpu.VMEM((GZ, CX + 2, SLAB + 32, CZ), jnp.bfloat16),
            pltpu.VMEM((GZ, CX, SLAB + 16, CZ), jnp.int32),
            pltpu.VMEM((GZ, CX, 4), jnp.float32),
            pltpu.SMEM((3, MATS), jnp.float32),
            pltpu.SMEM((MATS,), jnp.float32),
            pltpu.SMEM((MATS,), jnp.float32),
            pltpu.SMEM((1, 5), jnp.int32),
            pltpu.VMEM((GZ, 16, 8, 128), jnp.float32),
            pltpu.VMEM((5, 8, 128), jnp.float32),
            pltpu.VMEM((16, SLAB + 8, 2 * CZ), jnp.float32),
            pltpu.VMEM((2, 2, SLAB + 8, 2 * CZ), jnp.float32),
            pltpu.VMEM((5, SLAB, 2 * CZ), jnp.float32),
            pltpu.VMEM((16, 32, CZ), jnp.bfloat16),
            pltpu.VMEM((GX, 32, CZ), jnp.bfloat16),
            pltpu.SemaphoreType.DMA((8,)),
            pltpu.SemaphoreType.DMA((3,)),
            pltpu.SemaphoreType.DMA((3,)),
            pltpu.SemaphoreType.DMA((4,)),
            pltpu.SemaphoreType.DMA((4,)),
            pltpu.SemaphoreType.DMA((5,)),
            pltpu.SemaphoreType.DMA((2,)),
            pltpu.SemaphoreType.DMA((2,)),
            pltpu.SemaphoreType.DMA((4,)),
            pltpu.SemaphoreType.DMA,
            pltpu.SemaphoreType.DMA,
            pltpu.SemaphoreType.REGULAR((2,)),
            pltpu.SemaphoreType.REGULAR,
        ],
        compiler_params=pltpu.CompilerParams(
            collective_id=0, has_side_effects=True, vmem_limit_bytes=32 * 2**20
        ),
    )(*[
        pltpu.with_memory_space_constraint(x, pltpu.HBM)
        for x in (
            density, material, colour_table.T, opacity_table, centre_table, slice_weights,
            front_flags,
        )
    ])
    return frame.reshape(4, 1, 2048)


def solution(mesh):
    in_specs = (
        P("bricks", None, None, None),
        P("bricks", None, None, None),
        P(),
        P(),
        P(),
        P("bricks", None, None),
        P("bricks", None),
    )
    out_specs = P(None, "bricks", None)
    return jax.shard_map(body, mesh=mesh, in_specs=in_specs, out_specs=out_specs, check_vma=False)
```
